1024 devices in a mesh: expert: 32 (over y, x), tensor: 32 (over z, core).
Axes of the slice: x: 4, y: 8, z: 16, core: 2. Of those that a mesh axis runs over, the one named last changes fastest.
Arguments:
- hidden_in: bfloat16 [4096, 4096], P('expert'), may hold values from -6 to 6
- w_latent: bfloat16 [4096, 1024], P(None, 'tensor'), may hold values from -0.09375 to 0.09375
- routes: int32 [4096, 22], P('expert'), may hold values from 0 to 255, all different within a row; in each aligned block of 128 rows (0 to 127, 128 to 255, ...) at most 16 rows name the same one
- gates: float32 [4096, 22], P('expert'), may hold values from 0.05 to 1
- expert_gate: bfloat16 [1024, 1024, 336], P(('expert', 'tensor')), may hold values from -0.1875 to 0.1875
- expert_up: bfloat16 [1024, 1024, 336], P(('expert', 'tensor')), may hold values from -0.1875 to 0.1875
- expert_down: bfloat16 [1024, 336, 1024], P(('expert', 'tensor')), may hold values from -0.15625 to 0.15625
- shared_gate: bfloat16 [4096, 2688], P(None, 'tensor'), may hold values from -0.09375 to 0.09375
- shared_up: bfloat16 [4096, 2688], P(None, 'tensor'), may hold values from -0.09375 to 0.09375
- shared_down: bfloat16 [2688, 4096], P('tensor'), may hold values from -0.125 to 0.125
- w_restore: bfloat16 [1024, 4096], P('tensor'), may hold values from -0.1875 to 0.1875
Outputs:
- mixed: bfloat16 [4096, 4096], P(('expert', 'tensor'))
The draws below stay inside these ranges and needn't reach their ends.
Inputs may be any that keep to these rules, and one draw needn't show every extreme that they name: `routes`: each row names 22 different experts; among the 128 rows of one index of expert (aligned blocks), no expert is named more than 16 times.
All inputs are finite; a program needn't handle non-finite values.
Results may differ from the reference program's by a relative error of at most 0.03.
Values may be sent and summed in bfloat16 or wider, within the bound.
No kernel may reach another device: no remote copies, remote signals or barrier semaphores. Data moves between devices by JAX's collectives and lax.ppermute only.
A program may use at most 32 MiB of HBM per device.

```python
import math
import jax
import jax.numpy as jnp
import numpy as np
from jax import lax

D = 4096
LAT = 1024
FE = 1344
FS = 2688
TOK_GRP = 128
EXPERTS = 256
TOP = 22
CAP = 16
TOKENS = 4096
N_EXPERT = 32


def block_scale(rng, dims, split, smallest, top_value):
    level = 1.0
    for dim, parts in split:
        draws = jax.random.uniform(jax.random.fold_in(jax.random.fold_in(rng, 6), dim), (parts,), jnp.float32, smallest / len(split), top_value / len(split))
        level = level * jnp.repeat(jnp.exp(draws), dims[dim] // parts).reshape((-1,) + (1,) * (len(dims) - 1 - dim))
    return level


def assign_block(rng, own, number, rows, count, top, most, lean):
    ranking = jax.random.permutation(rng, count)
    crowded, ordinary = shares(count, rows * top, most, lean, True), shares(count, rows * top, most, lean, False)
    places = jnp.arange(count)

    def named(tallies, rotation):
        used = int((tallies > 0).sum())
        fixed = max(1, used // 4)
        moved = fixed + (places - fixed + rotation * (used - fixed)) % max(1, count - fixed)
        return jnp.zeros((count,), jnp.int32).at[ranking[jnp.where(places < fixed, places, moved)]].set(jnp.asarray(tallies, jnp.int32))

    tallies = jnp.where(number % 4 == 0, named(crowded, number // 4), named(ordinary, number - number // 4 - 1))
    mixed = jax.random.permutation(jax.random.fold_in(own, 3), count)
    giver, receiver = mixed[0:count // 2 * 2:2], mixed[1:count // 2 * 2:2]
    room = jnp.minimum(tallies[giver] - 1, most - tallies[receiver]) // 2
    room = jnp.where((giver == ranking[0]) | (receiver == ranking[0]) | (tallies[receiver] == 0), 0, jnp.maximum(room, 0))
    moved = jax.random.randint(jax.random.fold_in(own, 4), (count // 2,), 0, 1 << 20) % (room + 1)
    tallies = tallies.at[giver].add(-moved).at[receiver].add(moved)
    labels = jnp.searchsorted(jnp.cumsum(tallies), jnp.arange(rows * top), side="right").astype(jnp.int32)
    table = labels.reshape(top, rows).T
    table = table[jax.random.permutation(jax.random.fold_in(own, 1), rows)]
    rotation = jax.random.randint(jax.random.fold_in(own, 2), (rows, 1), 0, top)
    return jnp.take_along_axis(table, (jnp.arange(top)[None, :] + rotation) % top, axis=1)


def shares(amount, total, reach, slope, full):
    loads = [(1 << 20) // math.isqrt(grade ** slope) + 1 for grade in range(1, amount + 1)]
    largest = reach if full else min(reach, max(-(-total // amount), total * loads[0] // sum(loads)))
    least = 1 if total - largest >= amount - 1 else 0
    holding, spare = [largest] + [least] * (amount - 1), total - largest - least * (amount - 1)
    while spare > 0:
        candidates = [i for i in range(1, amount) if holding[i] < largest] or [i for i in range(1, amount) if holding[i] < reach]
        mass, remaining = sum([loads[i] for i in candidates]), spare
        for i in candidates:
            extra = min(reach - holding[i], max(1, remaining * loads[i] // mass), spare)
            holding[i] = holding[i] + extra
            spare = spare - extra
    return np.array(holding)


def centred(rng, extent, width, reach, split=(), kind=jnp.bfloat16):
    entries = jax.random.normal(rng, extent, jnp.float32) * width
    if len(split) > 0:
        entries = block_scale(rng, extent, split, -0.22, 0.18) * entries
    return jnp.clip(entries, min=-reach, max=reach).astype(kind)


def setup_inputs(seed: int = 0) -> dict:
    key_of = jax.random.split(jax.random.key(seed), 12)
    hidden_in = centred(key_of[0], (TOKENS, D), 1.0, 6.0, ((0, 32),))
    w_latent = centred(key_of[1], (D, LAT), D ** -0.5, 0.09375, ((1, 32),))
    routes_keys = jax.random.split(jax.random.fold_in(key_of[2], 1), TOKENS // TOK_GRP)
    routes_turns = jax.random.permutation(jax.random.fold_in(key_of[2], 3), TOKENS // TOK_GRP)
    routes = jax.vmap(lambda own, number: assign_block(jax.random.fold_in(key_of[2], 2), own, number, TOK_GRP, EXPERTS, TOP, CAP, 1))(routes_keys, routes_turns).reshape((TOKENS, TOP))
    gates = jnp.clip(0.05 + 0.95 * jax.random.uniform(key_of[3], (TOKENS, TOP), jnp.float32) ** block_scale(key_of[3], (TOKENS, TOP), ((0, 32),), -0.2, 0.2), 0.05, 1.0)
    expert_gate = centred(key_of[4], (4 * EXPERTS, LAT, FE // 4), LAT ** -0.5, 0.1875, ((0, 1024),))
    expert_up = centred(key_of[5], (4 * EXPERTS, LAT, FE // 4), LAT ** -0.5, 0.1875, ((0, 1024),))
    expert_down = centred(key_of[6], (4 * EXPERTS, FE // 4, LAT), FE ** -0.5, 0.15625, ((0, 1024),))
    shared_gate = centred(key_of[7], (D, FS), D ** -0.5, 0.09375, ((1, 32),))
    shared_up = centred(key_of[8], (D, FS), D ** -0.5, 0.09375, ((1, 32),))
    shared_down = centred(key_of[9], (FS, D), FS ** -0.5, 0.125, ((0, 32),))
    w_restore = centred(key_of[10], (LAT, D), LAT ** -0.5, 0.1875, ((0, 32),))
    return dict(hidden_in=hidden_in, w_latent=w_latent, routes=routes, gates=gates, expert_gate=expert_gate, expert_up=expert_up, expert_down=expert_down, shared_gate=shared_gate, shared_up=shared_up, shared_down=shared_down, w_restore=w_restore)


def reference(hidden_in, w_latent, routes, gates, expert_gate, expert_up, expert_down, shared_gate, shared_up, shared_down, w_restore):
    latent = jnp.dot(hidden_in, w_latent, preferred_element_type=jnp.float32).astype(jnp.bfloat16)
    row_ids = jnp.arange(TOKENS, dtype=jnp.int32)
    hit_count = jnp.zeros((TOKENS, EXPERTS), jnp.int32).at[row_ids[:, None], routes].add(1)
    grouped = hit_count.reshape(N_EXPERT, TOK_GRP, EXPERTS)
    slot_of = (jnp.cumsum(grouped, axis=1) - grouped).reshape(TOKENS, EXPERTS).astype(jnp.int32)
    slot_pick = jnp.take_along_axis(slot_of, routes, axis=1).astype(jnp.int32)
    group_of = (row_ids // TOK_GRP).astype(jnp.int32)
    row_grid = jnp.broadcast_to(row_ids[:, None], routes.shape).astype(jnp.int32)
    group_grid = jnp.broadcast_to(group_of[:, None], routes.shape).astype(jnp.int32)
    slot_rows = jnp.full((EXPERTS, N_EXPERT, CAP), TOKENS, jnp.int32).at[routes, group_grid, slot_pick].set(row_grid)
    slot_gates = jnp.zeros((EXPERTS, N_EXPERT, CAP), jnp.float32).at[routes, group_grid, slot_pick].set(gates)
    padded = jnp.concatenate([latent, jnp.zeros((1, LAT), jnp.bfloat16)], axis=0)

    def expert_step(accum_rows, expert_id):
        row_index = slot_rows[expert_id].reshape(-1)
        taken = padded[row_index]
        output_sum = jnp.zeros((N_EXPERT * CAP, LAT), jnp.float32)
        for quarter in range(4):
            which = 4 * expert_id + quarter
            gate_act = jnp.dot(taken, expert_gate[which], preferred_element_type=jnp.float32)
            up_act = jnp.dot(taken, expert_up[which], preferred_element_type=jnp.float32)
            hidden_act = (jax.nn.silu(gate_act) * up_act).astype(jnp.bfloat16)
            part = jnp.dot(hidden_act, expert_down[which], preferred_element_type=jnp.float32).astype(jnp.bfloat16)
            output_sum = output_sum + part.astype(jnp.float32)
        weighted = output_sum * slot_gates[expert_id].reshape(-1)[:, None]
        return accum_rows.at[row_index].add(weighted), None

    start_rows = jnp.zeros((TOKENS + 1, LAT), jnp.float32)
    accum_rows, _ = lax.scan(expert_step, start_rows, jnp.arange(EXPERTS, dtype=jnp.int32))
    routed = accum_rows[:TOKENS].astype(jnp.bfloat16)
    shared_gate_act = jnp.dot(hidden_in, shared_gate, preferred_element_type=jnp.float32)
    shared_up_act = jnp.dot(hidden_in, shared_up, preferred_element_type=jnp.float32)
    shared_act = (jax.nn.silu(shared_gate_act) * shared_up_act).astype(jnp.bfloat16)
    total = jnp.dot(shared_act, shared_down, preferred_element_type=jnp.float32) + jnp.dot(routed, w_restore, preferred_element_type=jnp.float32)
    return total.astype(jnp.bfloat16)
```

```python
import jax
import jax.numpy as jnp
from jax import lax
from jax.sharding import Mesh, PartitionSpec as P

TENSOR = ("z", "c")
BF16 = jnp.bfloat16
F32 = jnp.float32


def dot(a, b):
    return jnp.dot(a, b, preferred_element_type=F32)


def swap_cores(value):
    return lax.ppermute(value, "c", [(0, 1), (1, 0)])


def shards(
    hidden_in,
    w_latent,
    routes,
    gates,
    expert_gate,
    expert_up,
    expert_down,
    shared_gate,
    shared_up,
    shared_down,
    w_restore,
):
    groups = lax.axis_size("expert")
    chips = lax.axis_size("z")
    cores = lax.axis_size("c")
    tensor_size = chips * cores
    core = lax.axis_index("c")
    position = lax.axis_index("z") * cores + core
    rows = hidden_in.shape[0]
    block = w_restore.shape[0]
    width = block * tensor_size
    model = hidden_in.shape[1]
    top = routes.shape[1]
    experts = groups * tensor_size // 4
    capacity = 4 * max(1, 3 * rows * top // (8 * experts))

    latent_cols = dot(hidden_in, w_latent).astype(BF16)
    copies = jnp.broadcast_to(latent_cols.T[None], (tensor_size, block, rows))
    latent_t = lax.all_to_all(copies, TENSOR, 0, 0, tiled=True).reshape(width, rows)

    targets = jnp.arange(groups, dtype=jnp.int32) * (tensor_size // 4) + position // 4
    matched = routes[:, :, None] == targets[None, None, :]
    hits = jnp.sum(matched.astype(BF16), axis=1)
    weight = jnp.sum(jnp.where(matched, gates[:, :, None], 0.0), axis=1)
    below = (
        lax.broadcasted_iota(jnp.int32, (rows, rows), 0)
        > lax.broadcasted_iota(jnp.int32, (rows, rows), 1)
    ).astype(BF16)
    earlier = dot(below, hits)
    slots = jnp.where(hits > 0.5, earlier, -1.0).T
    slot_ids = jnp.arange(capacity, dtype=F32)
    slot_mask = slots[:, None, :] == slot_ids[None, :, None]
    pick = slot_mask.astype(BF16).reshape(groups * capacity, rows)
    weighted = jnp.where(slot_mask, weight.T[:, None, :], 0.0).reshape(groups * capacity, rows)
    weighted_high = weighted.astype(BF16)
    weighted_low = (weighted - weighted_high.astype(F32)).astype(BF16)

    outbound = lax.dot_general(
        pick, latent_t, (((1,), (1,)), ((), ())), preferred_element_type=F32
    ).astype(BF16)
    taken = lax.all_to_all(
        outbound.reshape(groups, capacity, width), "expert", 0, 0, tiled=True
    ).reshape(groups * capacity, width)
    gate_act = dot(taken, expert_gate[0])
    up_act = dot(taken, expert_up[0])
    act = (jax.nn.silu(gate_act) * up_act).astype(BF16)
    part = dot(act, expert_down[0]).astype(BF16)
    returned = lax.all_to_all(
        part.reshape(groups, capacity, width), "expert", 0, 0, tiled=True
    ).reshape(groups * capacity, width)

    def combine(w):
        return lax.dot_general(
            returned, w, (((0,), (0,)), ((), ())), preferred_element_type=F32
        )

    routed_terms = (combine(weighted_high) + combine(weighted_low)).astype(BF16)
    pieces = lax.all_to_all(
        routed_terms.reshape(tensor_size, block, rows), TENSOR, 0, 0, tiled=True
    )
    routed_t = jnp.sum(pieces.astype(F32), axis=0).astype(BF16)

    shared_act = (jax.nn.silu(dot(hidden_in, shared_gate)) * dot(hidden_in, shared_up)).astype(BF16)
    total = dot(shared_act, shared_down) + lax.dot_general(
        routed_t, w_restore, (((0,), (0,)), ((), ())), preferred_element_type=F32
    )
    own = rows // tensor_size
    by_core = total.reshape(chips, cores, own, model)
    keep = jnp.where(core == 0, by_core[:, 0], by_core[:, 1])
    give = jnp.where(core == 0, by_core[:, 1], by_core[:, 0]).astype(BF16)
    pair = (keep + swap_cores(give).astype(F32)).astype(BF16)
    final = lax.all_to_all(pair, "z", 0, 0, tiled=True)
    return jnp.sum(final.astype(F32), axis=0).astype(BF16)


def solution(mesh):
    shape = mesh.devices.shape
    split = Mesh(mesh.devices.reshape(shape[0], shape[1] // 2, 2), ("expert", "z", "c"))
    both = ("expert", "z", "c")
    in_specs = (
        P("expert", None),
        P(None, TENSOR),
        P("expert", None),
        P("expert", None),
        P(both, None, None),
        P(both, None, None),
        P(both, None, None),
        P(None, TENSOR),
        P(None, TENSOR),
        P(TENSOR, None),
        P(TENSOR, None),
    )
    return jax.shard_map(
        shards, mesh=split, in_specs=in_specs, out_specs=P(both, None), check_vma=False
    )
```

```python
import jax
import jax.numpy as jnp
from jax import lax
from jax.sharding import Mesh, PartitionSpec as P

CHIPS = ("i", "j", "k", "b")
TENSOR = CHIPS + ("c",)
BF16 = jnp.bfloat16
F32 = jnp.float32


def dot(a, b):
    return jnp.dot(a, b, preferred_element_type=F32)


def swap(value, axis):
    return lax.ppermute(value, axis, [(0, 1), (1, 0)])


def swap_cores(value):
    return swap(value, "c")


def fold(value, axis):
    me = lax.axis_index(axis)
    both = value.reshape((value.shape[0] // 2, 2) + value.shape[1:])
    given = swap(jnp.where(me == 0, both[:, 1], both[:, 0]).astype(BF16), axis)
    return jnp.where(me == 0, both[:, 0], both[:, 1]) + given.astype(F32)


def shards(
    hidden_in,
    w_latent,
    routes,
    gates,
    expert_gate,
    expert_up,
    expert_down,
    shared_gate,
    shared_up,
    shared_down,
    w_restore,
):
    groups = lax.axis_size("expert")
    chips = lax.axis_size(CHIPS)
    cores = lax.axis_size("c")
    tensor_size = chips * cores
    core = lax.axis_index("c")
    position = lax.axis_index(TENSOR)
    rows = hidden_in.shape[0]
    block = w_restore.shape[0]
    width = block * tensor_size
    model = hidden_in.shape[1]
    top = routes.shape[1]
    experts = groups * tensor_size // 4
    capacity = 4 * max(1, 3 * rows * top // (8 * experts))

    half = block * chips

    own = rows // tensor_size
    wide = model // cores
    restore = lax.all_gather(
        jnp.pad(w_restore, ((0, 0), (0, 1024))), CHIPS, axis=0, tiled=True
    )

    latent_cols = dot(hidden_in, w_latent).astype(BF16)
    copies = jnp.broadcast_to(latent_cols.T[None], (chips, block, rows))
    latent_t = lax.all_to_all(copies, CHIPS, 0, 0, tiled=True).reshape(half, rows)

    place = lax.broadcasted_iota(jnp.int32, (half, width), 0)
    column = lax.broadcasted_iota(jnp.int32, (half, width), 1)
    first = (place // block) * (cores * block) + place % block

    def choose(which):
        return (column == first + which * block).astype(BF16)

    mine, theirs = choose(core), choose(1 - core)

    targets = jnp.arange(groups, dtype=jnp.int32) * (tensor_size // 4) + position // 4
    matched = routes[:, :, None] == targets[None, None, :]
    hits = jnp.sum(matched.astype(BF16), axis=1)
    below = (
        lax.broadcasted_iota(jnp.int32, (rows, rows), 0)
        > lax.broadcasted_iota(jnp.int32, (rows, rows), 1)
    ).astype(BF16)
    earlier = dot(below, hits)
    slots = jnp.where(hits > 0.5, earlier, -1.0).T
    slot_ids = jnp.arange(capacity, dtype=F32)
    slot_mask = slots[:, None, :] == slot_ids[None, :, None]
    pick = slot_mask.astype(BF16).reshape(groups * capacity, rows)

    gate = [dot(m, expert_gate[0]).astype(BF16) for m in (mine, theirs)]
    latent_t, gate = lax.optimization_barrier((latent_t, gate))
    gate_mine, gate_theirs = gate
    outbound = lax.dot_general(
        pick, latent_t, (((1,), (1,)), ((), ())), preferred_element_type=F32
    ).astype(BF16)
    outbound, expert_up, expert_down = lax.optimization_barrier(
        (outbound, expert_up, expert_down)
    )
    taken = lax.all_to_all(
        outbound.reshape(groups, capacity, half), "expert", 0, 0, tiled=True
    ).reshape(groups * capacity, half)

    up = [dot(m, expert_up[0]).astype(BF16) for m in (mine, theirs)]
    down = [dot(expert_down[0], m.T).astype(BF16) for m in (mine, theirs)]
    shared_act = (
        jax.nn.silu(dot(hidden_in, shared_gate)) * dot(hidden_in, shared_up)
    ).astype(BF16)
    total = dot(shared_act, shared_down)
    left, right = total[:, :wide], total[:, wide:]
    given = swap_cores(jnp.where(core == 0, right, left).astype(BF16))
    pair = jnp.where(core == 0, left, right) + given.astype(F32)
    folded = fold(pair.reshape(chips, cores * own, wide), "b")
    taken, up, down = lax.optimization_barrier((taken, up, down))
    up_mine, up_theirs = up
    down_mine, down_theirs = down
    other = swap_cores(taken)
    gate_act = dot(taken, gate_mine) + dot(other, gate_theirs)
    up_act = dot(taken, up_mine) + dot(other, up_theirs)
    act = (jax.nn.silu(gate_act) * up_act).astype(BF16)
    received = swap_cores(dot(act, down_theirs).astype(BF16))
    part = (dot(act, down_mine) + received.astype(F32)).astype(BF16)
    part, routes_later, folded = lax.optimization_barrier((part, routes, folded))
    returned = lax.all_to_all(
        part.reshape(groups, capacity, half), "expert", 0, 0, tiled=True
    ).reshape(groups * capacity, half)

    folded = fold(folded, "k")
    folded = fold(folded, "j")
    matched = routes_later[:, :, None] == targets[None, None, :]
    weight = jnp.sum(jnp.where(matched, gates[:, :, None], 0.0), axis=1)
    weighted = jnp.where(slot_mask, weight.T[:, None, :], 0.0).reshape(groups * capacity, rows)
    weighted_high = weighted.astype(BF16)
    weighted_low = (weighted - weighted_high.astype(F32)).astype(BF16)
    returned, restore, folded, weighted_high, weighted_low = lax.optimization_barrier(
        (returned, restore, folded, weighted_high, weighted_low)
    )

    def combine(w):
        return lax.dot_general(
            w, returned, (((0,), (0,)), ((), ())), preferred_element_type=F32
        )

    routed_terms = (combine(weighted_high) + combine(weighted_low)).astype(BF16)
    pieces = lax.all_to_all(
        routed_terms.reshape(chips, cores * own, half), CHIPS, 0, 0, tiled=True
    )
    routed = jnp.sum(pieces.astype(F32), axis=0).astype(BF16)
    shared_sum = fold(folded, "i")[0]
    restored = dot(routed, restore)[:, :model]
    blank = jnp.zeros_like(shared_sum)
    both = restored + jnp.concatenate(
        [jnp.where(core == 0, shared_sum, blank), jnp.where(core == 0, blank, shared_sum)], axis=1
    )
    kept = jnp.where(core == 0, both[:own], both[own:])
    given = swap_cores(jnp.where(core == 0, both[own:], both[:own]).astype(BF16))
    return (kept + given.astype(F32)).astype(BF16)


def solution(mesh):
    shape = mesh.devices.shape
    split = Mesh(
        mesh.devices.reshape((shape[0],) + (2,) * len(TENSOR)), ("expert",) + TENSOR
    )
    both = ("expert",) + TENSOR
    in_specs = (
        P("expert", None),
        P(None, TENSOR),
        P("expert", None),
        P("expert", None),
        P(both, None, None),
        P(both, None, None),
        P(both, None, None),
        P(None, TENSOR),
        P(None, TENSOR),
        P(TENSOR, None),
        P(TENSOR, None),
    )
    return jax.shard_map(
        shards, mesh=split, in_specs=in_specs, out_specs=P(both, None), check_vma=False
    )
```

```python
import jax
import jax.numpy as jnp
from jax import lax
from jax.sharding import Mesh, PartitionSpec as P

CHIPS = ("i", "j", "k", "b")
TENSOR = CHIPS + ("c",)
BF16 = jnp.bfloat16
F32 = jnp.float32


def dot(a, b):
    return jnp.dot(a, b, preferred_element_type=F32)


def swap(value, axis):
    return lax.ppermute(value, axis, [(0, 1), (1, 0)])


def swap_cores(value):
    return swap(value, "c")


def shards(
    hidden_in,
    w_latent,
    routes,
    gates,
    expert_gate,
    expert_up,
    expert_down,
    shared_gate,
    shared_up,
    shared_down,
    w_restore,
):
    groups = lax.axis_size("expert")
    chips = lax.axis_size(CHIPS)
    cores = lax.axis_size("c")
    tensor_size = chips * cores
    core = lax.axis_index("c")
    position = lax.axis_index(TENSOR)
    rows = hidden_in.shape[0]
    block = w_restore.shape[0]
    width = block * tensor_size
    model = hidden_in.shape[1]
    top = routes.shape[1]
    experts = groups * tensor_size // 4
    capacity = 4 * max(1, 3 * rows * top // (8 * experts))

    half = block * chips

    own = rows // tensor_size
    wide = model // cores
    restore = lax.all_gather(
        jnp.pad(w_restore, ((0, 0), (0, 512))), CHIPS, axis=0, tiled=True
    )

    latent_cols = dot(hidden_in, w_latent).astype(BF16)
    copies = jnp.broadcast_to(latent_cols.T[None], (chips, block, rows))
    latent_t = lax.all_to_all(copies, CHIPS, 0, 0, tiled=True).reshape(half, rows)

    place = lax.broadcasted_iota(jnp.int32, (half, width), 0)
    column = lax.broadcasted_iota(jnp.int32, (half, width), 1)
    first = (place // block) * (cores * block) + place % block

    def choose(which):
        return (column == first + which * block).astype(BF16)

    mine, theirs = choose(core), choose(1 - core)

    targets = jnp.arange(groups, dtype=jnp.int32) * (tensor_size // 4) + position // 4
    matched = routes[:, :, None] == targets[None, None, :]
    hits = jnp.sum(matched.astype(BF16), axis=1)
    below = (
        lax.broadcasted_iota(jnp.int32, (rows, rows), 0)
        > lax.broadcasted_iota(jnp.int32, (rows, rows), 1)
    ).astype(BF16)
    earlier = dot(below, hits)
    slots = jnp.where(hits > 0.5, earlier, -1.0).T
    slot_ids = jnp.arange(capacity, dtype=F32)
    slot_mask = slots[:, None, :] == slot_ids[None, :, None]
    pick = slot_mask.astype(BF16).reshape(groups * capacity, rows)

    gate = [dot(m, expert_gate[0]).astype(BF16) for m in (mine, theirs)]
    latent_t, gate = lax.optimization_barrier((latent_t, gate))
    gate_mine, gate_theirs = gate
    outbound = lax.dot_general(
        pick, latent_t, (((1,), (1,)), ((), ())), preferred_element_type=F32
    ).astype(BF16)
    outbound, expert_up, expert_down = lax.optimization_barrier(
        (outbound, expert_up, expert_down)
    )
    taken = lax.all_to_all(
        outbound.reshape(groups, capacity, half), "expert", 0, 0, tiled=True
    ).reshape(groups * capacity, half)

    up = [dot(m, expert_up[0]).astype(BF16) for m in (mine, theirs)]
    down = [dot(expert_down[0], m.T).astype(BF16) for m in (mine, theirs)]
    shared_act = (
        jax.nn.silu(dot(hidden_in, shared_gate)) * dot(hidden_in, shared_up)
    ).astype(BF16)
    total = dot(shared_act, shared_down)
    left, right = total[:, :wide], total[:, wide:]
    given = swap_cores(jnp.where(core == 0, right, left).astype(BF16))
    pair = jnp.where(core == 0, left, right) + given.astype(F32)
    pair = pair.astype(BF16)
    taken, up, down, pair = lax.optimization_barrier((taken, up, down, pair))
    shared_sum = lax.psum_scatter(pair, CHIPS, scatter_dimension=0, tiled=True)
    up_mine, up_theirs = up
    down_mine, down_theirs = down
    other = swap_cores(taken)
    gate_act = dot(taken, gate_mine) + dot(other, gate_theirs)
    up_act = dot(taken, up_mine) + dot(other, up_theirs)
    act = (jax.nn.silu(gate_act) * up_act).astype(BF16)
    received = swap_cores(dot(act, down_theirs).astype(BF16))
    part = (dot(act, down_mine) + received.astype(F32)).astype(BF16)
    part, routes_later = lax.optimization_barrier((part, routes))
    returned = lax.all_to_all(
        part.reshape(groups, capacity, half), "expert", 0, 0, tiled=True
    ).reshape(groups * capacity, half)

    matched = routes_later[:, :, None] == targets[None, None, :]
    weight = jnp.sum(jnp.where(matched, gates[:, :, None], 0.0), axis=1)
    weighted = jnp.where(slot_mask, weight.T[:, None, :], 0.0).reshape(groups * capacity, rows)
    weighted_high = weighted.astype(BF16)
    weighted_low = (weighted - weighted_high.astype(F32)).astype(BF16)
    returned, restore, weighted_high, weighted_low = lax.optimization_barrier(
        (returned, restore, weighted_high, weighted_low)
    )

    def combine(w):
        return lax.dot_general(
            w, returned, (((0,), (0,)), ((), ())), preferred_element_type=F32
        )

    routed_terms = (combine(weighted_high) + combine(weighted_low)).astype(BF16)
    pieces = lax.all_to_all(
        routed_terms.reshape(chips, cores * own, half), CHIPS, 0, 0, tiled=True
    )
    routed = jnp.sum(pieces.astype(F32), axis=0).astype(BF16)
    shared_sum = shared_sum.astype(F32)
    restored = dot(routed, restore)[:, :model]
    blank = jnp.zeros_like(shared_sum)
    both = restored + jnp.concatenate(
        [jnp.where(core == 0, shared_sum, blank), jnp.where(core == 0, blank, shared_sum)], axis=1
    )
    kept = jnp.where(core == 0, both[:own], both[own:])
    given = swap_cores(jnp.where(core == 0, both[own:], both[:own]).astype(BF16))
    return (kept + given.astype(F32)).astype(BF16)


def solution(mesh):
    shape = mesh.devices.shape
    split = Mesh(
        mesh.devices.reshape((shape[0],) + (2,) * len(TENSOR)), ("expert",) + TENSOR
    )
    both = ("expert",) + TENSOR
    in_specs = (
        P("expert", None),
        P(None, TENSOR),
        P("expert", None),
        P("expert", None),
        P(both, None, None),
        P(both, None, None),
        P(both, None, None),
        P(None, TENSOR),
        P(None, TENSOR),
        P(TENSOR, None),
        P(TENSOR, None),
    )
    return jax.shard_map(
        shards, mesh=split, in_specs=in_specs, out_specs=P(both, None), check_vma=False
    )
```
